32 devices in a mesh: tm: 8 (over y, x, core), tile: 4 (over z).
Axes of the slice: x: 2, y: 2, z: 4, core: 2. Of those that a mesh axis runs over, the one named last changes fastest.
Arguments:
- movie: bfloat16 [32, 256, 1024], P('tm', 'tile'), may hold values from -6 to 6
- lift_weight: float32 [24], replicated, may hold values from -4 to 4
- lift_bias: float32 [24], replicated, may hold values from -3 to 3
- depth_kernel: float32 [3, 24, 9], replicated, may hold values from -2 to 2
- mix_weight: bfloat16 [3, 24, 24], replicated, may hold values from -1.25 to 1.25
- mix_bias: float32 [3, 24], replicated, may hold values from -3 to 3
- out_weight: float32 [24], replicated, may hold values from -1.25 to 1.25
- temporal_kernel: float32 [9], replicated, may hold values from -2 to 2
- footprints: bfloat16 [256, 256, 1024], P(None, 'tile', 'tm'), may hold values from -0.0625 to 0.0625
- slot_owner: int32 [8192, 1], P(('tm', 'tile')), may hold values from 0 to 31; in each aligned block of 256 rows (0 to 255, 256 to 511, ...) at most 16 rows name the same one
- slot_neuron: int32 [8192], P(('tm', 'tile')), may hold values from 0 to 319
Outputs:
- filtered: bfloat16 [32, 256, 1024], P(None, 'tile', 'tm')
- traces: float32 [10240, 32], P(('tm', 'tile'))
The draws below stay inside these ranges and needn't reach their ends.
Inputs may be any that keep to these rules, and one draw needn't show every extreme that they name: `slot_owner`: within the rows of one device (256 aligned rows), no owner is named more than 16 times.
All inputs are finite; a program needn't handle non-finite values.
Results may differ from the reference program's by a relative error of at most 0.012.
Values may be sent and summed in bfloat16 or wider, within the bound.
A program may use at most 128 MiB of HBM per device.

```python
import math
import jax
import jax.numpy as jnp
import numpy as np
from jax import lax

C = 24
LAYERS = 3
KT = 9
ROWS_DEV = 64
COLS_DEV = 128
SLOTS_DEV = 256
NEUR_DEV = 320
FRAMES = 32
H = 256
W = 1024
NEURONS = 10240
CAP = 16
N_TM = 8
N_TILE = 4


def with_ends(values, own_key, least, top_value):
    dims = values.shape
    place = [jax.random.randint(jax.random.fold_in(own_key, axis), (), 0, dims[axis]) for axis in range(len(dims))]
    values = values.at[tuple(place)].set(least)
    longest = dims.index(max(dims))
    place[longest] = (place[longest] + 1) % dims[longest]
    return values.at[tuple(place)].set(top_value)


def steps_of(own_key, dims, pieces, smallest, high):
    loudness, own = 1.0, jax.random.fold_in(own_key, 6)
    for dim, shards_of in pieces:
        heights = jnp.exp(jax.random.uniform(jax.random.fold_in(own, dim), (shards_of,), jnp.float32, smallest / len(pieces), high / len(pieces)))
        loudness = loudness * jnp.repeat(heights, dims[dim] // shards_of).reshape([-1 if axis == dim else 1 for axis in range(len(dims))])
    return loudness


def deal_out(own_key, own, number, rows, number_of, top, most, skew):
    order = jax.random.permutation(own_key, number_of)
    heavy_load, ordinary = portions_of(number_of, rows * top, most, skew, True), portions_of(number_of, rows * top, most, skew, False)
    places = jnp.arange(number_of)

    def named(tallies, turn):
        used = int((tallies > 0).sum())
        fixed = max(1, used // 4)
        moved = fixed + (places - fixed + turn * (used - fixed)) % max(1, number_of - fixed)
        return jnp.zeros((number_of,), jnp.int32).at[order[jnp.where(places < fixed, places, moved)]].set(jnp.asarray(tallies, jnp.int32))

    tallies = jnp.where(number % 4 == 0, named(heavy_load, number // 4), named(ordinary, number - number // 4 - 1))
    mixed = jax.random.permutation(jax.random.fold_in(own, 3), number_of)
    donor, receiver = mixed[0:number_of // 2 * 2:2], mixed[1:number_of // 2 * 2:2]
    room = jnp.minimum(tallies[donor] - 1, most - tallies[receiver]) // 2
    room = jnp.where((donor == order[0]) | (receiver == order[0]) | (tallies[receiver] == 0), 0, jnp.maximum(room, 0))
    moved = jax.random.randint(jax.random.fold_in(own, 4), (number_of // 2,), 0, 1 << 20) % (room + 1)
    tallies = tallies.at[donor].add(-moved).at[receiver].add(moved)
    members = jnp.searchsorted(jnp.cumsum(tallies), jnp.arange(rows * top), side="right").astype(jnp.int32)
    table = members.reshape(top, rows).T
    table = table[jax.random.permutation(jax.random.fold_in(own, 1), rows)]
    turn = jax.random.randint(jax.random.fold_in(own, 2), (rows, 1), 0, top)
    return jnp.take_along_axis(table, (jnp.arange(top)[None, :] + turn) % top, axis=1)


def portions_of(count, total, bound, lean, full):
    portions = [(1 << 20) // math.isqrt(grade ** lean) + 1 for grade in range(1, count + 1)]
    largest = bound if full else min(bound, max(-(-total // count), total * portions[0] // sum(portions)))
    least = 1 if total - largest >= count - 1 else 0
    holding, surplus = [largest] + [least] * (count - 1), total - largest - least * (count - 1)
    while surplus > 0:
        candidates = [i for i in range(1, count) if holding[i] < largest] or [i for i in range(1, count) if holding[i] < bound]
        mass, budget = sum([portions[i] for i in candidates]), surplus
        for i in candidates:
            addition = min(bound - holding[i], max(1, budget * portions[i] // mass), surplus)
            holding[i] = holding[i] + addition
            surplus = surplus - addition
    return np.array(holding)


def normal_values(rng, shape, width, reach, split=(), kind=jnp.bfloat16):
    factor_of = steps_of(rng, shape, split, -0.22, 0.18) if split else 1.0
    entries = jax.random.normal(rng, shape, jnp.float32) * width * factor_of
    return jnp.minimum(jnp.maximum(entries, -reach), reach).astype(kind)


def setup_inputs(seed: int = 0) -> dict:
    key_of = jax.random.split(jax.random.key(seed), 12)
    movie = normal_values(key_of[0], (FRAMES, H, W), 1.0, 6.0, ((0, 8), (1, 4)))
    lift_weight = normal_values(key_of[1], (C,), 1.0, 4.0, (), jnp.float32)
    lift_bias = normal_values(key_of[2], (C,), 0.5, 3.0, (), jnp.float32)
    depth_kernel = normal_values(key_of[3], (LAYERS, C, 9), 9 ** -0.5, 2.0, (), jnp.float32)
    mix_weight = normal_values(key_of[4], (LAYERS, C, C), C ** -0.5, 1.25)
    mix_bias = normal_values(key_of[5], (LAYERS, C), 0.5, 3.0, (), jnp.float32)
    out_weight = normal_values(key_of[6], (C,), C ** -0.5, 1.25, (), jnp.float32)
    temporal_kernel = normal_values(key_of[7], (KT,), KT ** -0.5, 2.0, (), jnp.float32)
    footprints = normal_values(key_of[8], (SLOTS_DEV, H, W), (ROWS_DEV * COLS_DEV) ** -0.5, 0.0625, ((1, 4), (2, 8)))
    slot_owner_keys = jax.random.split(jax.random.fold_in(key_of[9], 1), (N_TM * N_TILE * SLOTS_DEV) // SLOTS_DEV)
    slot_owner_turns = jax.random.permutation(jax.random.fold_in(key_of[9], 3), (N_TM * N_TILE * SLOTS_DEV) // SLOTS_DEV)
    slot_owner = jax.vmap(lambda own, number: deal_out(jax.random.fold_in(key_of[9], 2), own, number, SLOTS_DEV, N_TM * N_TILE, 1, CAP, 2))(slot_owner_keys, slot_owner_turns).reshape((N_TM * N_TILE * SLOTS_DEV, 1))
    slot_neuron = with_ends(jax.random.randint(key_of[10], (N_TM * N_TILE * SLOTS_DEV,), 0, NEUR_DEV), jax.random.fold_in(key_of[10], 1), 0, NEUR_DEV - 1).astype(jnp.int32)
    return dict(movie=movie, lift_weight=lift_weight, lift_bias=lift_bias, depth_kernel=depth_kernel, mix_weight=mix_weight, mix_bias=mix_bias, out_weight=out_weight, temporal_kernel=temporal_kernel, footprints=footprints, slot_owner=slot_owner, slot_neuron=slot_neuron)


def depthwise(features, kernel):
    row_count = features.shape[1]
    col_count = features.shape[2]
    padded = jnp.pad(features, ((0, 0), (1, 1), (1, 1)))
    summed = jnp.zeros(features.shape, jnp.float32)
    for row_shift in range(3):
        for col_shift in range(3):
            weight_tap = kernel[:, row_shift * 3 + col_shift][:, None, None]
            summed = summed + weight_tap * padded[:, row_shift:row_shift + row_count, col_shift:col_shift + col_count]
    return summed


def reference(movie, lift_weight, lift_bias, depth_kernel, mix_weight, mix_bias, out_weight, temporal_kernel, footprints, slot_owner, slot_neuron):
    def denoise_frame(frame):
        frame_f32 = frame.astype(jnp.float32)
        features = (lift_weight[:, None, None] * frame_f32[None] + lift_bias[:, None, None]).astype(jnp.bfloat16)
        for depth_step in range(LAYERS):
            spread = depthwise(features.astype(jnp.float32), depth_kernel[depth_step]).astype(jnp.bfloat16)
            mixed_sum = jnp.einsum("cd,chw->dhw", mix_weight[depth_step].astype(jnp.float32), spread.astype(jnp.float32), precision=lax.Precision.HIGHEST)
            mixed_sum = mixed_sum + mix_bias[depth_step][:, None, None]
            features = (features.astype(jnp.float32) + jnp.maximum(mixed_sum, 0.0)).astype(jnp.bfloat16)
        projected = jnp.sum(out_weight[:, None, None] * features.astype(jnp.float32), axis=0)
        return (frame_f32 + projected).astype(jnp.bfloat16)

    denoised = lax.map(denoise_frame, movie)
    half_taps = KT // 2
    padded = jnp.pad(denoised.astype(jnp.float32), ((half_taps, half_taps), (0, 0), (0, 0)))
    summed = jnp.zeros((FRAMES, H, W), jnp.float32)
    for tap_index in range(KT):
        summed = summed + temporal_kernel[tap_index] * padded[tap_index:tap_index + FRAMES]
    filtered = summed.astype(jnp.bfloat16)

    filtered_blocks = filtered.astype(jnp.float32).reshape(FRAMES, N_TILE, ROWS_DEV, N_TM, COLS_DEV)

    def slot_term(footprint):
        blocks = footprint.astype(jnp.float32).reshape(N_TILE, ROWS_DEV, N_TM, COLS_DEV)
        return jnp.einsum("jric,fjric->ijf", blocks, filtered_blocks, precision=lax.Precision.HIGHEST)

    partial_value = lax.map(slot_term, footprints)
    partial_value = jnp.transpose(partial_value, (1, 2, 0, 3)).reshape(N_TM * N_TILE * SLOTS_DEV, FRAMES)
    neuron_ids = (slot_owner[:, 0] * NEUR_DEV + slot_neuron).astype(jnp.int32)
    traces = jax.ops.segment_sum(partial_value, neuron_ids, num_segments=NEURONS)
    return filtered, traces
```

```python
import jax
import jax.numpy as jnp
from jax import lax
from jax.experimental import pallas as pl
from jax.experimental.pallas import tpu as pltpu
from jax.sharding import PartitionSpec as P

LAYERS = 3
NEUR_DEV = 320
LANES = 128
ROWS_DOT = 4
PAD = 8


def split_halves(values):
    high = lax.reduce_precision(values, 8, 7)
    return high.astype(jnp.bfloat16), (values - high).astype(jnp.bfloat16)


def banded(taps, rows_out, rows_in, offset):
    out_row = jnp.arange(rows_out)[:, None, None]
    in_row = jnp.arange(rows_in)[None, :, None]
    hit = (in_row == out_row + offset + jnp.arange(3)[None, None, :]).astype(jnp.float32)
    extra = taps.ndim - 1
    hit = hit.reshape(hit.shape + (1,) * extra)
    return jnp.sum(hit * taps[None, None], axis=2)


def layer_weights(kernel, mixing):
    channels = mixing.shape[0]
    taps = kernel.reshape(channels, 3, 3).transpose(1, 2, 0)[:, :, :, None] * mixing.astype(
        jnp.float32
    )
    band = banded(taps, ROWS_DOT, ROWS_DOT + 2, 0)
    band = band.transpose(0, 4, 2, 1, 3)
    return band.reshape(ROWS_DOT * channels, 3 * (ROWS_DOT + 2) * channels).astype(jnp.bfloat16)


def first_weights(kernel, mixing, lift_weight, lift_bias):
    channels = mixing.shape[0]
    taps = kernel.reshape(channels, 3, 3).transpose(1, 2, 0)[:, :, :, None] * mixing.astype(
        jnp.float32
    )
    pieces = []
    for lift in (lift_weight, lift_bias):
        summed = jnp.sum(taps * lift[None, None, :, None], axis=2)
        band = banded(summed, 8, 16, 5).transpose(0, 3, 2, 1)
        pieces.extend(split_halves(band.reshape(8 * channels, 48)))
    return jnp.concatenate(pieces, axis=1)


def denoise_kernel(
    movie_ref,
    perm_ref,
    first_ref,
    second_ref,
    third_ref,
    lift_ref,
    bias_ref,
    out_ref,
    result_ref,
    frames_buf,
    inside_buf,
    feat1,
    feat2,
    den_buf,
):
    frames = movie_ref.shape[0]
    high = movie_ref.shape[1]
    width = movie_ref.shape[2]
    rows = high - 2 * PAD
    channels = lift_ref.shape[0]
    tiles = width // LANES
    chunk = 2 * LANES
    tile_index = lax.axis_index("tile")
    tile_count = lax.axis_size("tile")
    lane = lax.broadcasted_iota(jnp.int32, (1, LANES), 1)

    def store_edges(ref, where, low, top):
        ref[where, 0:LANES] = jnp.where(lane == 0, 0.0, pltpu.roll(top, 1, 1)).astype(ref.dtype)
        ref[where, (tiles + 1) * LANES : (tiles + 2) * LANES] = jnp.where(
            lane == LANES - 1, 0.0, pltpu.roll(low, LANES - 1, 1)
        ).astype(ref.dtype)

    flat = movie_ref[...].reshape(frames * high, width)
    permuted = jnp.dot(flat, perm_ref[...], preferred_element_type=jnp.float32)
    frames_buf[:, LANES : LANES + width] = permuted
    store_edges(
        frames_buf, slice(0, frames * high), permuted[:, :LANES], permuted[:, width - LANES :]
    )
    row = lax.broadcasted_iota(jnp.int32, (high, width + 2 * LANES), 0) - PAD
    col = lax.broadcasted_iota(jnp.int32, (high, width + 2 * LANES), 1)
    row = row + tile_index * rows
    keep = (row >= 0) & (row < rows * tile_count)
    keep = keep & (col != 0) & (col != width + 2 * LANES - 1)
    inside_buf[...] = jnp.where(keep, 1.0, 0.0)

    groups1 = (rows + 2 * (LAYERS - 1) + 7) // 8
    lift_w = lift_ref[:, 0:1]
    lift_b = lift_ref[:, 1:2]

    def first_group(frame, group):
        base = pl.multiple_of(frame * high + group * 8, 8)
        inner = pl.multiple_of(group * 8, 8)
        target = pl.multiple_of(group * (8 * channels), 16)
        bias = bias_ref[0]
        ends = {}
        for start in range(0, width, chunk):
            parts = [
                frames_buf[pl.ds(base, 16), start + j * LANES : start + j * LANES + chunk]
                for j in range(3)
            ]
            masks = [
                inside_buf[pl.ds(inner, 16), start + j * LANES : start + j * LANES + chunk]
                for j in range(3)
            ]
            window = parts[1]
            parts = [part.astype(jnp.bfloat16) for part in parts]
            masks = [mask.astype(jnp.bfloat16) for mask in masks]
            stack = jnp.concatenate(parts + parts + masks + masks, axis=0)
            mixed = jnp.dot(first_ref[...], stack, preferred_element_type=jnp.float32)
            lifted = jnp.concatenate(
                [lift_w * window[o + 6 : o + 7] + lift_b for o in range(8)], axis=0
            )
            value = lifted + jnp.maximum(mixed + bias, 0.0)
            feat1[pl.ds(target, 8 * channels), LANES + start : LANES + start + chunk] = (
                value.astype(jnp.bfloat16)
            )
            if start == 0:
                ends["low"] = value[:, :LANES]
            if start + chunk == width:
                ends["top"] = value[:, chunk - LANES :]
        store_edges(feat1, pl.ds(target, 8 * channels), ends["low"], ends["top"])

    def layer_rows(ref, weights_ref, bias, source, start):
        depth = (ROWS_DOT + 2) * channels
        parts = [
            ref[pl.ds(source, depth), start + j * LANES : start + j * LANES + chunk]
            for j in range(3)
        ]
        centre = parts[1].astype(jnp.float32)[channels : (ROWS_DOT + 1) * channels]
        stack = jnp.concatenate(parts, axis=0)
        mixed = jnp.dot(weights_ref[...], stack, preferred_element_type=jnp.float32)
        return centre + jnp.maximum(mixed + bias, 0.0)

    span = ROWS_DOT * channels

    def second_group(group):
        target = pl.multiple_of(group * span, 16)
        bias = bias_ref[1][:span]
        ends = {}
        for start in range(0, width, chunk):
            value = layer_rows(feat1, second_ref, bias, target, start)
            feat2[pl.ds(target, span), LANES + start : LANES + start + chunk] = value.astype(
                jnp.bfloat16
            )
            if start == 0:
                ends["low"] = value[:, :LANES]
            if start + chunk == width:
                ends["top"] = value[:, chunk - LANES :]
        store_edges(feat2, pl.ds(target, span), ends["low"], ends["top"])

    def third_group(frame, group):
        base = pl.multiple_of(frame * high + PAD + group * 8, 8)
        target = pl.multiple_of(frame * rows + group * 8, 8)
        bias = bias_ref[2][:span]
        out_weight = out_ref[:span]
        for start in range(0, width, chunk):
            sums = []
            for half in range(8 // ROWS_DOT):
                source = pl.multiple_of(group * (8 * channels) + half * span, 16)
                value = layer_rows(feat2, third_ref, bias, source, start) * out_weight
                sums.append(jnp.sum(value.reshape(ROWS_DOT, channels, chunk), axis=1))
            projected = jnp.concatenate(sums, axis=0) if len(sums) > 1 else sums[0]
            movie = frames_buf[pl.ds(base, 8), LANES + start : LANES + start + chunk]
            den_buf[pl.ds(target, 8), start : start + chunk] = movie + projected

    groups2 = -(-(rows + 2) // ROWS_DOT)
    zero_from = groups1 * 8 * channels
    if feat1.shape[0] > zero_from:
        feat1[zero_from:, :] = jnp.zeros((feat1.shape[0] - zero_from, feat1.shape[1]), jnp.bfloat16)

    def one_frame(frame, carry):
        def run1(group, inner):
            first_group(frame, group)
            return inner

        lax.fori_loop(0, groups1, run1, 0, unroll=3 if groups1 % 3 == 0 else 1)

        @pl.when(tile_index == 0)
        def _():
            feat1[0 : 2 * channels, :] = jnp.zeros((2 * channels, feat1.shape[1]), jnp.bfloat16)

        @pl.when(tile_index == tile_count - 1)
        def _():
            lower = (rows + 2) * channels
            feat1[lower : lower + 2 * channels, :] = jnp.zeros(
                (2 * channels, feat1.shape[1]), jnp.bfloat16
            )

        def run2(group, inner):
            second_group(group)
            return inner

        lax.fori_loop(0, groups2, run2, 0, unroll=4)

        def clear(lower, count):
            first = lower // 16 * 16
            size = -(-(lower + count) // 16) * 16 - first
            at = lax.broadcasted_iota(jnp.int32, (size, feat2.shape[1]), 0) + first
            old = feat2[first : first + size, :].astype(jnp.float32)
            outside = (at >= lower) & (at < lower + count)
            feat2[first : first + size, :] = jnp.where(outside, 0.0, old).astype(jnp.bfloat16)

        @pl.when(tile_index == 0)
        def _():
            clear(0, channels)

        @pl.when(tile_index == tile_count - 1)
        def _():
            clear((rows + 1) * channels, channels)

        def run3(group, inner):
            third_group(frame, group)
            return inner

        lax.fori_loop(0, rows // 8, run3, 0, unroll=2)
        return carry

    lax.fori_loop(0, frames, one_frame, 0)
    restored = lax.dot_general(
        den_buf[...].astype(jnp.bfloat16),
        perm_ref[...],
        (((1,), (1,)), ((), ())),
        preferred_element_type=jnp.float32,
    )
    result_ref[...] = restored.astype(jnp.bfloat16).reshape(frames, rows, width)


def denoise(movie, lift_weight, lift_bias, depth_kernel, mix_weight, mix_bias, out_weight):
    frames, rows, width = movie.shape
    channels = lift_weight.shape[0]
    count = lax.axis_size("tile")
    forward = [(i, i + 1) for i in range(count - 1)]
    backward = [(target, source) for source, target in forward]
    low = lax.ppermute(movie[:, rows - LAYERS :], "tile", forward)
    top = lax.ppermute(movie[:, :LAYERS], "tile", backward)
    blank = jnp.zeros((frames, PAD - LAYERS, width), movie.dtype)
    widened = jnp.concatenate([blank, low, movie, top, blank], axis=1)
    tiles = width // LANES
    place = jnp.arange(width)
    perm = (place[:, None] == (place % LANES * tiles + place // LANES)[None, :]).astype(
        jnp.bfloat16
    )
    first = first_weights(depth_kernel[0], mix_weight[0], lift_weight, lift_bias)
    second = layer_weights(depth_kernel[1], mix_weight[1])
    third = layer_weights(depth_kernel[2], mix_weight[2])
    lift = jnp.stack([lift_weight, lift_bias], axis=1)
    bias = jnp.tile(mix_bias, (1, 8))[:, :, None]
    out_col = jnp.tile(out_weight, 8)[:, None]
    groups1 = (rows + 2 * (LAYERS - 1) + 7) // 8
    groups2 = -(-(rows + 2) // ROWS_DOT)
    rows1 = max(groups1 * 8, groups2 * ROWS_DOT + 2)
    rows2 = groups2 * ROWS_DOT
    wide = width + 2 * LANES
    high = rows + 2 * PAD
    return pl.pallas_call(
        denoise_kernel,
        out_shape=jax.ShapeDtypeStruct(movie.shape, jnp.bfloat16),
        in_specs=[pl.BlockSpec(memory_space=pltpu.VMEM)] * 8,
        out_specs=pl.BlockSpec(memory_space=pltpu.VMEM),
        scratch_shapes=[
            pltpu.VMEM((frames * high, wide), jnp.float32),
            pltpu.VMEM((high, wide), jnp.float32),
            pltpu.VMEM((rows1 * channels, wide), jnp.bfloat16),
            pltpu.VMEM((rows2 * channels, wide), jnp.bfloat16),
            pltpu.VMEM((frames * rows, width), jnp.float32),
        ],
        compiler_params=pltpu.CompilerParams(vmem_limit_bytes=40 * 1024 * 1024),
    )(widened, perm, first, second, third, lift, bias, out_col)


def temporal(received, temporal_kernel):
    frame_count = received.shape[0]
    tap_count = temporal_kernel.shape[0]
    half_taps = tap_count // 2
    padded = jnp.pad(received.astype(jnp.float32), ((half_taps, half_taps), (0, 0), (0, 0)))
    summed = jnp.zeros(received.shape, jnp.float32)
    for tap_index in range(tap_count):
        summed = summed + temporal_kernel[tap_index] * padded[tap_index : tap_index + frame_count]
    return summed.astype(jnp.bfloat16)


def local(
    movie,
    lift_weight,
    lift_bias,
    depth_kernel,
    mix_weight,
    mix_bias,
    out_weight,
    temporal_kernel,
    footprints,
    slot_owner,
    slot_neuron,
):
    denoised = denoise(
        movie, lift_weight, lift_bias, depth_kernel, mix_weight, mix_bias, out_weight
    )
    filtered = temporal(
        lax.all_to_all(denoised, "tm", split_axis=2, concat_axis=0, tiled=True), temporal_kernel
    )
    frame_total, block_rows, block_cols = filtered.shape
    slot_total = footprints.shape[0]
    partial_value = lax.dot_general(
        footprints.reshape(slot_total, block_rows * block_cols),
        filtered.reshape(frame_total, block_rows * block_cols),
        (((1,), (1,)), ((), ())),
        preferred_element_type=jnp.float32,
    )
    tm_count = lax.axis_size("tm")
    tile_count = lax.axis_size("tile")
    device_count = tm_count * tile_count
    capacity = max(4, 2 * slot_total // device_count)
    target = slot_owner[:, 0]
    chosen = (target[:, None] == jnp.arange(device_count, dtype=jnp.int32)[None, :]).astype(
        jnp.int32
    )
    earlier = jnp.cumsum(chosen, axis=0) - chosen
    position = target * capacity + jnp.sum(earlier * chosen, axis=1)
    outgoing = (
        jnp.zeros((device_count * capacity, frame_total), jnp.float32)
        .at[position]
        .set(partial_value)
    )
    outgoing_ids = jnp.zeros((device_count * capacity,), jnp.int32).at[position].set(slot_neuron)
    arriving, arriving_ids = (
        lax.all_to_all(
            outgoing.reshape(device_count, capacity, frame_total).astype(jnp.bfloat16),
            ("tm", "tile"),
            split_axis=0,
            concat_axis=0,
            tiled=True,
        ).astype(jnp.float32),
        lax.all_to_all(
            outgoing_ids.reshape(device_count, capacity),
            ("tm", "tile"),
            split_axis=0,
            concat_axis=0,
            tiled=True,
        ),
    )
    arriving = arriving.reshape(device_count * capacity, frame_total)
    arriving_ids = arriving_ids.reshape(device_count * capacity)
    traces = jax.ops.segment_sum(arriving, arriving_ids, num_segments=NEUR_DEV)
    return (filtered, traces)


def solution(mesh):
    return jax.shard_map(
        local,
        mesh=mesh,
        in_specs=(
            P("tm", "tile", None),
            P(),
            P(),
            P(),
            P(),
            P(),
            P(),
            P(),
            P(None, "tile", "tm"),
            P(("tm", "tile"), None),
            P(("tm", "tile")),
        ),
        out_specs=(P(None, "tile", "tm"), P(("tm", "tile"), None)),
        check_vma=False,
    )
```

```python
import functools

import jax
import jax.numpy as jnp
from jax import lax
from jax.experimental import pallas as pl
from jax.experimental.pallas import tpu as pltpu
from jax.sharding import PartitionSpec as P

LAYERS = 3
NEUR_DEV = 320
LANES = 128
ROWS_DOT = 4
PAD = 8


EXACT = lax.Precision.HIGHEST


def exact_dot(left, right, dims):
    return lax.dot_general(
        left, right, (dims, ((), ())), precision=EXACT, preferred_element_type=jnp.float32
    )


def one_hot(shape, hit):
    first = lax.broadcasted_iota(jnp.int32, shape, 0)
    second = lax.broadcasted_iota(jnp.int32, shape, 1)
    return jnp.where(hit(first, second), 1.0, 0.0)


def layer_weights(kernel, mixing):
    channels = mixing.shape[0]
    span = ROWS_DOT * channels
    depth = (ROWS_DOT + 2) * channels
    spread_rows = one_hot((span, channels), lambda r, d: r % channels == d)
    spread_cols = one_hot((channels, 3 * depth), lambda c, s: s % channels == c)
    by_row = lax.dot_general(
        spread_rows.astype(jnp.bfloat16),
        mixing,
        (((1,), (1,)), ((), ())),
        preferred_element_type=jnp.float32,
    ).astype(jnp.bfloat16)
    mixed = jnp.dot(by_row, spread_cols.astype(jnp.bfloat16), preferred_element_type=jnp.float32)
    taps = exact_dot(kernel, spread_cols, ((0,), (0,)))
    tap = lax.broadcasted_iota(jnp.int32, (9, 3 * depth), 0)
    shift = lax.broadcasted_iota(jnp.int32, (9, 3 * depth), 1) // depth
    out_row = lax.broadcasted_iota(jnp.int32, (span, 3 * depth), 0) // channels
    in_row = lax.broadcasted_iota(jnp.int32, (span, 3 * depth), 1) % depth // channels
    total = jnp.zeros((span, 3 * depth), jnp.float32)
    for i in range(3):
        chosen = jnp.sum(jnp.where(tap == 3 * i + shift, taps, 0.0), axis=0, keepdims=True)
        total = total + jnp.where(in_row == out_row + i, chosen, 0.0)
    return (total * mixed).astype(jnp.bfloat16)


def first_weights(kernel, mixing, lift_pair):
    channels = mixing.shape[0]
    mixing = mixing.astype(jnp.float32)
    spread_rows = one_hot((8 * channels, channels), lambda r, d: r % channels == d)
    out_row = lax.broadcasted_iota(jnp.int32, (8 * channels, 48), 0) // channels
    in_row = lax.broadcasted_iota(jnp.int32, (8 * channels, 48), 1) % 16
    pieces = []
    for which in range(2):
        gathered = exact_dot(mixing, kernel * lift_pair[:, which : which + 1], ((0,), (0,)))
        gathered = exact_dot(spread_rows, gathered, ((1,), (0,)))
        total = jnp.zeros((8 * channels, 48), jnp.float32)
        for i in range(3):
            pick = one_hot((9, 48), lambda tap, s: tap == 3 * i + s // 16)
            term = exact_dot(gathered, pick, ((1,), (0,)))
            total = total + jnp.where(in_row == out_row + 5 + i, term, 0.0)
        high = total.astype(jnp.bfloat16)
        pieces += [high, (total - high.astype(jnp.float32)).astype(jnp.bfloat16)]
    return jnp.concatenate([piece.astype(jnp.float32) for piece in pieces], axis=1).astype(
        jnp.bfloat16
    )


def denoise_kernel(
    movie_ref,
    low_ref,
    top_ref,
    lift_weight_ref,
    lift_bias_ref,
    depth_ref,
    mix_ref,
    mix_bias_ref,
    out_weight_ref,
    result_ref,
    perm_ref,
    first_ref,
    second_ref,
    third_ref,
    params_ref,
    frames_buf,
    inside_buf,
    feat1,
    feat2,
    den_buf,
):
    frames, rows, width = movie_ref.shape
    high = rows + 2 * PAD
    channels = lift_weight_ref.shape[1]
    tiles = width // LANES
    chunk = 2 * LANES
    tile_index = lax.axis_index("tile")
    tile_count = lax.axis_size("tile")
    lane = lax.broadcasted_iota(jnp.int32, (1, LANES), 1)

    def store_edges(ref, where, low, top):
        ref[where, 0:LANES] = jnp.where(lane == 0, 0.0, pltpu.roll(top, 1, 1)).astype(ref.dtype)
        ref[where, (tiles + 1) * LANES : (tiles + 2) * LANES] = jnp.where(
            lane == LANES - 1, 0.0, pltpu.roll(low, LANES - 1, 1)
        ).astype(ref.dtype)

    wide_place = lax.broadcasted_iota(jnp.int32, (1, width), 1)
    source_col = wide_place % LANES * tiles + wide_place // LANES

    def build(block, carry):
        at = lax.broadcasted_iota(jnp.int32, (LANES, width), 0) + block * LANES
        perm_ref[pl.ds(pl.multiple_of(block * LANES, LANES), LANES), :] = jnp.where(
            at == source_col, 1.0, 0.0
        ).astype(jnp.bfloat16)
        return carry

    lax.fori_loop(0, tiles, build, 0)
    params = jnp.concatenate(
        [lift_weight_ref[...], lift_bias_ref[...], out_weight_ref[...], mix_bias_ref[...]], axis=0
    )
    spread_rows = one_hot((8 * channels, channels), lambda r, d: r % channels == d)
    params_ref[...] = exact_dot(spread_rows, params, ((1,), (1,)))
    lift_pair = params_ref[:channels, 0:2]
    first_ref[...] = first_weights(depth_ref[0], mix_ref[0], lift_pair)
    second_ref[...] = layer_weights(depth_ref[1], mix_ref[1])
    third_ref[...] = layer_weights(depth_ref[2], mix_ref[2])
    pieces = []
    for frame in range(frames):
        blank = jnp.zeros((PAD - LAYERS, width), jnp.float32)
        low = low_ref[frame].astype(jnp.float32)
        top = top_ref[frame].astype(jnp.float32)
        pieces += [
            jnp.concatenate([blank, low], axis=0),
            movie_ref[frame].astype(jnp.float32),
            jnp.concatenate([top, blank], axis=0),
        ]
    flat = jnp.concatenate(pieces, axis=0).astype(jnp.bfloat16)
    permuted = jnp.dot(flat, perm_ref[...], preferred_element_type=jnp.float32)
    frames_buf[:, LANES : LANES + width] = permuted
    store_edges(
        frames_buf, slice(0, frames * high), permuted[:, :LANES], permuted[:, width - LANES :]
    )
    row = lax.broadcasted_iota(jnp.int32, (high, width + 2 * LANES), 0) - PAD
    col = lax.broadcasted_iota(jnp.int32, (high, width + 2 * LANES), 1)
    row = row + tile_index * rows
    keep = (row >= 0) & (row < rows * tile_count)
    keep = keep & (col != 0) & (col != width + 2 * LANES - 1)
    inside_buf[...] = jnp.where(keep, 1.0, 0.0)

    groups1 = (rows + 2 * (LAYERS - 1) + 7) // 8
    lift_w = params_ref[:channels, 0:1]
    lift_b = params_ref[:channels, 1:2]

    def first_group(frame, group):
        base = pl.multiple_of(frame * high + group * 8, 8)
        inner = pl.multiple_of(group * 8, 8)
        target = pl.multiple_of(group * (8 * channels), 16)
        bias = params_ref[:, 3:4]
        ends = {}
        for start in range(0, width, chunk):
            parts = [
                frames_buf[pl.ds(base, 16), start + j * LANES : start + j * LANES + chunk]
                for j in range(3)
            ]
            masks = [
                inside_buf[pl.ds(inner, 16), start + j * LANES : start + j * LANES + chunk]
                for j in range(3)
            ]
            window = parts[1]
            parts = [part.astype(jnp.bfloat16) for part in parts]
            masks = [mask.astype(jnp.bfloat16) for mask in masks]
            stack = jnp.concatenate(parts + parts + masks + masks, axis=0)
            mixed = jnp.dot(first_ref[...], stack, preferred_element_type=jnp.float32)
            lifted = jnp.concatenate(
                [lift_w * window[o + 6 : o + 7] + lift_b for o in range(8)], axis=0
            )
            value = lifted + jnp.maximum(mixed + bias, 0.0)
            feat1[pl.ds(target, 8 * channels), LANES + start : LANES + start + chunk] = (
                value.astype(jnp.bfloat16)
            )
            if start == 0:
                ends["low"] = value[:, :LANES]
            if start + chunk == width:
                ends["top"] = value[:, chunk - LANES :]
        store_edges(feat1, pl.ds(target, 8 * channels), ends["low"], ends["top"])

    def layer_rows(ref, weights_ref, bias, source, start):
        depth = (ROWS_DOT + 2) * channels
        parts = [
            ref[pl.ds(source, depth), start + j * LANES : start + j * LANES + chunk]
            for j in range(3)
        ]
        centre = parts[1].astype(jnp.float32)[channels : (ROWS_DOT + 1) * channels]
        stack = jnp.concatenate(parts, axis=0)
        mixed = jnp.dot(weights_ref[...], stack, preferred_element_type=jnp.float32)
        return centre + jnp.maximum(mixed + bias, 0.0)

    span = ROWS_DOT * channels

    def second_group(group):
        target = pl.multiple_of(group * span, 16)
        bias = params_ref[:span, 4:5]
        ends = {}
        for start in range(0, width, chunk):
            value = layer_rows(feat1, second_ref, bias, target, start)
            feat2[pl.ds(target, span), LANES + start : LANES + start + chunk] = value.astype(
                jnp.bfloat16
            )
            if start == 0:
                ends["low"] = value[:, :LANES]
            if start + chunk == width:
                ends["top"] = value[:, chunk - LANES :]
        store_edges(feat2, pl.ds(target, span), ends["low"], ends["top"])

    def third_group(frame, group):
        base = pl.multiple_of(frame * high + PAD + group * 8, 8)
        target = pl.multiple_of(frame * rows + group * 8, 8)
        bias = params_ref[:span, 5:6]
        out_weight = params_ref[:span, 2:3]
        for start in range(0, width, chunk):
            sums = []
            for half in range(8 // ROWS_DOT):
                source = pl.multiple_of(group * (8 * channels) + half * span, 16)
                value = layer_rows(feat2, third_ref, bias, source, start) * out_weight
                sums.append(jnp.sum(value.reshape(ROWS_DOT, channels, chunk), axis=1))
            projected = jnp.concatenate(sums, axis=0) if len(sums) > 1 else sums[0]
            movie = frames_buf[pl.ds(base, 8), LANES + start : LANES + start + chunk]
            den_buf[pl.ds(target, 8), start : start + chunk] = movie + projected

    groups2 = -(-(rows + 2) // ROWS_DOT)
    zero_from = groups1 * 8 * channels
    if feat1.shape[0] > zero_from:
        feat1[zero_from:, :] = jnp.zeros((feat1.shape[0] - zero_from, feat1.shape[1]), jnp.bfloat16)

    def one_frame(frame, carry):
        def run1(group, inner):
            first_group(frame, group)
            return inner

        lax.fori_loop(0, groups1, run1, 0, unroll=3 if groups1 % 3 == 0 else 1)

        @pl.when(tile_index == 0)
        def _():
            feat1[0 : 2 * channels, :] = jnp.zeros((2 * channels, feat1.shape[1]), jnp.bfloat16)

        @pl.when(tile_index == tile_count - 1)
        def _():
            lower = (rows + 2) * channels
            feat1[lower : lower + 2 * channels, :] = jnp.zeros(
                (2 * channels, feat1.shape[1]), jnp.bfloat16
            )

        def run2(group, inner):
            second_group(group)
            return inner

        lax.fori_loop(0, groups2, run2, 0, unroll=4)

        def clear(lower, count):
            first = lower // 16 * 16
            size = -(-(lower + count) // 16) * 16 - first
            at = lax.broadcasted_iota(jnp.int32, (size, feat2.shape[1]), 0) + first
            old = feat2[first : first + size, :].astype(jnp.float32)
            outside = (at >= lower) & (at < lower + count)
            feat2[first : first + size, :] = jnp.where(outside, 0.0, old).astype(jnp.bfloat16)

        @pl.when(tile_index == 0)
        def _():
            clear(0, channels)

        @pl.when(tile_index == tile_count - 1)
        def _():
            clear((rows + 1) * channels, channels)

        def run3(group, inner):
            third_group(frame, group)
            return inner

        lax.fori_loop(0, rows // 8, run3, 0, unroll=2)
        return carry

    lax.fori_loop(0, frames, one_frame, 0)
    restored = lax.dot_general(
        den_buf[...].astype(jnp.bfloat16),
        perm_ref[...],
        (((1,), (1,)), ((), ())),
        preferred_element_type=jnp.float32,
    )
    result_ref[...] = restored.astype(jnp.bfloat16).reshape(frames, rows, width)


def denoise(movie, lift_weight, lift_bias, depth_kernel, mix_weight, mix_bias, out_weight):
    frames, rows, width = movie.shape
    channels = lift_weight.shape[0]
    count = lax.axis_size("tile")
    forward = [(i, i + 1) for i in range(count - 1)]
    backward = [(target, source) for source, target in forward]
    low = lax.ppermute(movie[:, rows - LAYERS :], "tile", forward)
    top = lax.ppermute(movie[:, :LAYERS], "tile", backward)
    groups1 = (rows + 2 * (LAYERS - 1) + 7) // 8
    groups2 = -(-(rows + 2) // ROWS_DOT)
    rows1 = max(groups1 * 8, groups2 * ROWS_DOT + 2)
    rows2 = groups2 * ROWS_DOT
    wide = width + 2 * LANES
    high = rows + 2 * PAD
    return pl.pallas_call(
        denoise_kernel,
        out_shape=jax.ShapeDtypeStruct(movie.shape, jnp.bfloat16),
        in_specs=[pl.BlockSpec(memory_space=pltpu.VMEM)] * 9,
        out_specs=pl.BlockSpec(memory_space=pltpu.VMEM),
        scratch_shapes=[
            pltpu.VMEM((width, width), jnp.bfloat16),
            pltpu.VMEM((8 * channels, 192), jnp.bfloat16),
            pltpu.VMEM((ROWS_DOT * channels, 3 * (ROWS_DOT + 2) * channels), jnp.bfloat16),
            pltpu.VMEM((ROWS_DOT * channels, 3 * (ROWS_DOT + 2) * channels), jnp.bfloat16),
            pltpu.VMEM((8 * channels, 6), jnp.float32),
            pltpu.VMEM((frames * high, wide), jnp.float32),
            pltpu.VMEM((high, wide), jnp.float32),
            pltpu.VMEM((rows1 * channels, wide), jnp.bfloat16),
            pltpu.VMEM((rows2 * channels, wide), jnp.bfloat16),
            pltpu.VMEM((frames * rows, width), jnp.float32),
        ],
        compiler_params=pltpu.CompilerParams(vmem_limit_bytes=40 * 1024 * 1024),
    )(
        movie,
        low,
        top,
        lift_weight[None],
        lift_bias[None],
        depth_kernel,
        mix_weight,
        mix_bias,
        out_weight[None],
    )


def trace_kernel(
    slot_capacity,
    denoised_ref,
    taps_ref,
    footprints_ref,
    owner_ref,
    neuron_ref,
    filtered_ref,
    traces_ref,
    received,
    padded,
    filtered_rows,
    filtered_flat,
    feet,
    feet_rows,
    feet_flat,
    outgoing,
    arriving,
    load_sem,
    own_sems,
    frame_send,
    frame_recv,
    trace_send,
    trace_recv,
):
    me_tm = lax.axis_index("tm")
    me_tile = lax.axis_index("tile")
    tm_count = lax.axis_size("tm")
    tile_count = lax.axis_size("tile")
    count = tm_count * tile_count
    me = me_tm * tile_count + me_tile
    frames = denoised_ref.shape[0]
    slots, rows, cols = feet.shape
    total, _, _ = received.shape
    half = taps_ref.shape[0] // 2

    load = pltpu.make_async_copy(footprints_ref, feet, load_sem)
    load.start()
    barrier = pltpu.get_barrier_semaphore()

    def greet(offset, carry):
        other = lax.rem(me + offset, count)
        pl.semaphore_signal(
            barrier,
            inc=1,
            device_id=(other // tile_count, lax.rem(other, tile_count)),
            device_id_type=pl.DeviceIdType.MESH,
        )
        return carry

    lax.fori_loop(1, count, greet, 0)
    pl.semaphore_wait(barrier, count - 1)

    def frame_copy(offset):
        other = lax.rem(me_tm + offset, tm_count)
        return pltpu.make_async_remote_copy(
            src_ref=denoised_ref.at[:, :, pl.ds(pl.multiple_of(other * cols, cols), cols)],
            dst_ref=received.at[pl.ds(me_tm * frames, frames)],
            send_sem=frame_send.at[offset],
            recv_sem=frame_recv.at[offset],
            device_id=(other, me_tile),
            device_id_type=pl.DeviceIdType.MESH,
        )

    own = pltpu.make_async_copy(
        denoised_ref.at[:, :, pl.ds(pl.multiple_of(me_tm * cols, cols), cols)],
        received.at[pl.ds(me_tm * frames, frames)],
        own_sems.at[0],
    )
    own.start()
    for offset in range(1, tm_count):
        frame_copy(offset).start()

    load.wait()

    def widen(block, carry):
        at = pl.multiple_of(block * 8, 8)
        feet_rows[pl.ds(pl.multiple_of(block * (8 * rows), 8 * rows), 8 * rows), :] = (
            feet[pl.ds(at, 8)].astype(jnp.float32).reshape(8 * rows, cols)
        )
        return carry

    lax.fori_loop(0, slots // 8, widen, 0, unroll=4)

    def flatten(row, carry):
        at = pl.multiple_of(row * cols, cols)
        feet_flat[:, pl.ds(at, cols)] = feet_rows[pl.ds(row, slots, stride=rows), :].astype(
            jnp.bfloat16
        )
        return carry

    lax.fori_loop(0, rows, flatten, 0, unroll=4)

    owner = owner_ref[...]
    device = lax.broadcasted_iota(jnp.int32, (slots, count), 1)
    chosen = jnp.where(owner == device, 1.0, 0.0)
    earlier = jnp.dot(
        one_hot((slots, slots), lambda s, other: other < s).astype(jnp.bfloat16),
        chosen.astype(jnp.bfloat16),
        preferred_element_type=jnp.float32,
    )
    rank = jnp.sum(earlier * chosen, axis=1, keepdims=True)
    place = owner.astype(jnp.float32) * float(slot_capacity) + rank
    spot = lax.broadcasted_iota(jnp.int32, (slots, count * slot_capacity), 1).astype(jnp.float32)
    packing = jnp.where(place == spot, 1.0, 0.0).astype(jnp.bfloat16)
    neuron = neuron_ref[...]
    digits_high = (neuron // 16).astype(jnp.float32)
    digits_low = (neuron % 16).astype(jnp.float32)

    for edge in (0, half + total):
        padded[edge : edge + half] = jnp.zeros((half, rows, cols), jnp.float32)
    own.wait()
    for offset in range(1, tm_count):
        frame_copy(offset).wait()

    def unpack(frame, carry):
        padded[frame + half] = received[frame].astype(jnp.float32)
        return carry

    lax.fori_loop(0, total, unpack, 0, unroll=4)
    taps = [taps_ref[tap] for tap in range(2 * half + 1)]

    def filter_frame(frame, carry):
        summed = taps[0] * padded[frame]
        for tap in range(1, 2 * half + 1):
            summed = summed + taps[tap] * padded[frame + tap]
        rounded = summed.astype(jnp.bfloat16)
        filtered_ref[frame] = rounded
        filtered_rows[pl.ds(pl.multiple_of(frame * rows, rows), rows), :] = rounded.astype(
            jnp.float32
        )
        return carry

    lax.fori_loop(0, total, filter_frame, 0, unroll=2)

    def flatten_frames(row, carry):
        at = pl.multiple_of(row * cols, cols)
        filtered_flat[:, pl.ds(at, cols)] = filtered_rows[
            pl.ds(row, total, stride=rows), :
        ].astype(jnp.bfloat16)
        return carry

    lax.fori_loop(0, rows, flatten_frames, 0, unroll=4)
    partial_value = lax.dot_general(
        feet_flat[...],
        filtered_flat[...],
        (((1,), (1,)), ((), ())),
        preferred_element_type=jnp.float32,
    )
    lane = lax.broadcasted_iota(jnp.int32, (slots, LANES), 1)
    wide = jnp.concatenate(
        [partial_value, jnp.zeros((slots, LANES - total), jnp.float32)], axis=1
    )
    wide = jnp.where(lane == total, digits_high, jnp.where(lane == total + 1, digits_low, wide))
    packed = lax.dot_general(
        packing,
        wide.astype(jnp.bfloat16),
        (((0,), (0,)), ((), ())),
        preferred_element_type=jnp.float32,
    )
    outgoing[...] = packed.astype(jnp.bfloat16).reshape(count, slot_capacity, LANES)

    def trace_copy(offset):
        other = lax.rem(me + offset, count)
        return pltpu.make_async_remote_copy(
            src_ref=outgoing.at[other],
            dst_ref=arriving.at[me],
            send_sem=trace_send.at[offset],
            recv_sem=trace_recv.at[offset],
            device_id=(other // tile_count, lax.rem(other, tile_count)),
            device_id_type=pl.DeviceIdType.MESH,
        )

    def send(offset, carry):
        trace_copy(offset).start()
        return carry

    lax.fori_loop(1, count, send, 0)
    own_traces = pltpu.make_async_copy(outgoing.at[me], arriving.at[me], own_sems.at[1])
    own_traces.start()
    own_traces.wait()

    def finish(offset, carry):
        trace_copy(offset).wait()
        return carry

    lax.fori_loop(1, count, finish, 0)
    gathered = arriving[...].reshape(count * slot_capacity, LANES)
    digits = gathered.astype(jnp.float32)
    index = digits[:, total : total + 1] * 16.0 + digits[:, total + 1 : total + 2]
    neurons = traces_ref.shape[0]
    wanted = lax.broadcasted_iota(jnp.int32, (count * slot_capacity, neurons), 1)
    member = jnp.where(index == wanted.astype(jnp.float32), 1.0, 0.0).astype(jnp.bfloat16)
    summed = lax.dot_general(
        member, gathered, (((0,), (0,)), ((), ())), preferred_element_type=jnp.float32
    )
    traces_ref[...] = summed[:, :total]


def local(
    movie,
    lift_weight,
    lift_bias,
    depth_kernel,
    mix_weight,
    mix_bias,
    out_weight,
    temporal_kernel,
    footprints,
    slot_owner,
    slot_neuron,
):
    denoised = denoise(
        movie, lift_weight, lift_bias, depth_kernel, mix_weight, mix_bias, out_weight
    )
    tm_count = lax.axis_size("tm")
    count = tm_count * lax.axis_size("tile")
    frames, rows, _ = movie.shape
    slots, _, cols = footprints.shape
    total = frames * tm_count
    slot_capacity = max(16, 2 * slots // count)
    half = temporal_kernel.shape[0] // 2
    vmem = pl.BlockSpec(memory_space=pltpu.VMEM)
    filtered, traces = pl.pallas_call(
        functools.partial(trace_kernel, slot_capacity),
        out_shape=(
            jax.ShapeDtypeStruct((total, rows, cols), jnp.bfloat16),
            jax.ShapeDtypeStruct((NEUR_DEV, total), jnp.float32),
        ),
        in_specs=[
            vmem,
            pl.BlockSpec(memory_space=pltpu.SMEM),
            pl.BlockSpec(memory_space=pl.ANY),
            vmem,
            vmem,
        ],
        out_specs=(vmem, vmem),
        scratch_shapes=[
            pltpu.VMEM((total, rows, cols), jnp.bfloat16),
            pltpu.VMEM((total + 2 * half, rows, cols), jnp.float32),
            pltpu.VMEM((total * rows, cols), jnp.float32),
            pltpu.VMEM((total, rows * cols), jnp.bfloat16),
            pltpu.VMEM((slots, rows, cols), jnp.bfloat16),
            pltpu.VMEM((slots * rows, cols), jnp.float32),
            pltpu.VMEM((slots, rows * cols), jnp.bfloat16),
            pltpu.VMEM((count, slot_capacity, LANES), jnp.bfloat16),
            pltpu.VMEM((count, slot_capacity, LANES), jnp.bfloat16),
            pltpu.SemaphoreType.DMA,
            pltpu.SemaphoreType.DMA((2,)),
            pltpu.SemaphoreType.DMA((tm_count,)),
            pltpu.SemaphoreType.DMA((tm_count,)),
            pltpu.SemaphoreType.DMA((count,)),
            pltpu.SemaphoreType.DMA((count,)),
        ],
        compiler_params=pltpu.CompilerParams(
            collective_id=0, has_side_effects=True, vmem_limit_bytes=44 * 1024 * 1024
        ),
    )(denoised, temporal_kernel, footprints, slot_owner, slot_neuron[:, None])
    return (filtered, traces)


def solution(mesh):
    return jax.shard_map(
        local,
        mesh=mesh,
        in_specs=(
            P("tm", "tile", None),
            P(),
            P(),
            P(),
            P(),
            P(),
            P(),
            P(),
            P(None, "tile", "tm"),
            P(("tm", "tile"), None),
            P(("tm", "tile")),
        ),
        out_specs=(P(None, "tile", "tm"), P(("tm", "tile"), None)),
        check_vma=False,
    )
```

```python
import functools

import jax
import jax.numpy as jnp
from jax import lax
from jax.experimental import pallas as pl
from jax.experimental.pallas import tpu as pltpu
from jax.sharding import PartitionSpec as P

LAYERS = 3
NEUR_DEV = 320
LANES = 128
ROWS_DOT = 8
HALO = 16
PAD = 8


EXACT = lax.Precision.HIGHEST


def exact_dot(left, right, dims):
    return lax.dot_general(
        left, right, (dims, ((), ())), precision=EXACT, preferred_element_type=jnp.float32
    )


def one_hot(shape, hit):
    first = lax.broadcasted_iota(jnp.int32, shape, 0)
    second = lax.broadcasted_iota(jnp.int32, shape, 1)
    return jnp.where(hit(first, second), 1.0, 0.0)


def layer_weights(kernel, mixing):
    channels = mixing.shape[0]
    span = ROWS_DOT * channels
    depth = (ROWS_DOT + 2) * channels
    spread_rows = one_hot((span, channels), lambda r, d: r % channels == d)
    spread_cols = one_hot((channels, 3 * depth), lambda c, s: s % channels == c)
    by_row = lax.dot_general(
        spread_rows.astype(jnp.bfloat16),
        mixing,
        (((1,), (1,)), ((), ())),
        preferred_element_type=jnp.float32,
    ).astype(jnp.bfloat16)
    mixed = jnp.dot(by_row, spread_cols.astype(jnp.bfloat16), preferred_element_type=jnp.float32)
    taps = exact_dot(kernel, spread_cols, ((1,), (0,)))
    tap = lax.broadcasted_iota(jnp.int32, (9, 3 * depth), 0)
    shift = lax.broadcasted_iota(jnp.int32, (9, 3 * depth), 1) // depth
    out_row = lax.broadcasted_iota(jnp.int32, (span, 3 * depth), 0) // channels
    in_row = lax.broadcasted_iota(jnp.int32, (span, 3 * depth), 1) % depth // channels
    total = jnp.zeros((span, 3 * depth), jnp.float32)
    for i in range(3):
        chosen = jnp.sum(jnp.where(tap == 3 * i + shift, taps, 0.0), axis=0, keepdims=True)
        total = total + jnp.where(in_row == out_row + i, chosen, 0.0)
    return (total * mixed).astype(jnp.bfloat16)


def first_weights(kernel, mixing, lift_pair):
    channels = mixing.shape[0]
    mixing = mixing.astype(jnp.float32)
    spread_rows = one_hot((8 * channels, channels), lambda r, d: r % channels == d)
    out_row = lax.broadcasted_iota(jnp.int32, (8 * channels, 48), 0) // channels
    in_row = lax.broadcasted_iota(jnp.int32, (8 * channels, 48), 1) % 16
    pieces = []
    for which in range(2):
        gathered = exact_dot(mixing, kernel * lift_pair[which : which + 1], ((0,), (1,)))
        gathered = exact_dot(spread_rows, gathered, ((1,), (0,)))
        total = jnp.zeros((8 * channels, 48), jnp.float32)
        for i in range(3):
            pick = one_hot((9, 48), lambda tap, s: tap == 3 * i + s // 16)
            term = exact_dot(gathered, pick, ((1,), (0,)))
            total = total + jnp.where(in_row == out_row + 5 + i, term, 0.0)
        high = total.astype(jnp.bfloat16)
        pieces += [high, (total - high.astype(jnp.float32)).astype(jnp.bfloat16)]
    return jnp.concatenate([piece.astype(jnp.float32) for piece in pieces], axis=1).astype(
        jnp.bfloat16
    )


def denoise_kernel(
    movie_ref,
    low_ref,
    top_ref,
    vectors_ref,
    mix_ref,
    result_ref,
    perm_ref,
    first_ref,
    second_ref,
    third_ref,
    params_ref,
    frames_buf,
    inside_buf,
    feat1,
    feat2,
    den_buf,
):
    frames, rows, width = movie_ref.shape
    high = rows + 2 * PAD
    channels = vectors_ref.shape[1]
    tiles = width // LANES
    chunk = 2 * LANES
    tile_index = lax.axis_index("tile")
    tile_count = lax.axis_size("tile")
    lane = lax.broadcasted_iota(jnp.int32, (1, LANES), 1)

    def store_edges(ref, where, low, top):
        ref[where, 0:LANES] = jnp.where(lane == 0, 0.0, pltpu.roll(top, 1, 1)).astype(ref.dtype)
        ref[where, (tiles + 1) * LANES : (tiles + 2) * LANES] = jnp.where(
            lane == LANES - 1, 0.0, pltpu.roll(low, LANES - 1, 1)
        ).astype(ref.dtype)

    wide_place = lax.broadcasted_iota(jnp.int32, (1, width), 1)
    source_col = wide_place % LANES * tiles + wide_place // LANES

    def build(block, carry):
        at = lax.broadcasted_iota(jnp.int32, (LANES, width), 0) + block * LANES
        perm_ref[pl.ds(pl.multiple_of(block * LANES, LANES), LANES), :] = jnp.where(
            at == source_col, 1.0, 0.0
        ).astype(jnp.bfloat16)
        return carry

    lax.fori_loop(0, tiles, build, 0)
    params = vectors_ref[0:8]
    spread_rows = one_hot((8 * channels, channels), lambda r, d: r % channels == d)
    params_ref[...] = exact_dot(spread_rows, params, ((1,), (1,)))
    first_ref[...] = first_weights(vectors_ref[8:17], mix_ref[0], params)
    second_ref[...] = layer_weights(vectors_ref[24:33], mix_ref[1])
    third_ref[...] = layer_weights(vectors_ref[40:49], mix_ref[2])
    has_low = jnp.where(tile_index > 0, 1.0, 0.0)
    has_top = jnp.where(tile_index < tile_count - 1, 1.0, 0.0)
    pieces = []
    for frame in range(frames):
        blank = jnp.zeros((PAD - LAYERS, width), jnp.float32)
        low = low_ref[frame].astype(jnp.float32)[HALO - LAYERS :] * has_low
        top = top_ref[frame].astype(jnp.float32)[:LAYERS] * has_top
        pieces += [
            jnp.concatenate([blank, low], axis=0),
            movie_ref[frame].astype(jnp.float32),
            jnp.concatenate([top, blank], axis=0),
        ]
    flat = jnp.concatenate(pieces, axis=0).astype(jnp.bfloat16)
    permuted = jnp.dot(flat, perm_ref[...], preferred_element_type=jnp.float32)
    frames_buf[:, LANES : LANES + width] = permuted
    store_edges(
        frames_buf, slice(0, frames * high), permuted[:, :LANES], permuted[:, width - LANES :]
    )
    row = lax.broadcasted_iota(jnp.int32, (high, width + 2 * LANES), 0) - PAD
    col = lax.broadcasted_iota(jnp.int32, (high, width + 2 * LANES), 1)
    row = row + tile_index * rows
    keep = (row >= 0) & (row < rows * tile_count)
    keep = keep & (col != 0) & (col != width + 2 * LANES - 1)
    inside_buf[...] = jnp.where(keep, 1.0, 0.0)

    groups1 = (rows + 2 * (LAYERS - 1) + 7) // 8
    lift_w = params_ref[:channels, 0:1]
    lift_b = params_ref[:channels, 1:2]

    def first_group(frame, group):
        base = pl.multiple_of(frame * high + group * 8, 8)
        inner = pl.multiple_of(group * 8, 8)
        target = pl.multiple_of(group * (8 * channels), 16)
        bias = params_ref[:, 3:4]
        ends = {}
        for start in range(0, width, chunk):
            parts = [
                frames_buf[pl.ds(base, 16), start + j * LANES : start + j * LANES + chunk]
                for j in range(3)
            ]
            masks = [
                inside_buf[pl.ds(inner, 16), start + j * LANES : start + j * LANES + chunk]
                for j in range(3)
            ]
            window = parts[1]
            parts = [part.astype(jnp.bfloat16) for part in parts]
            masks = [mask.astype(jnp.bfloat16) for mask in masks]
            stack = jnp.concatenate(parts + parts + masks + masks, axis=0)
            mixed = jnp.dot(first_ref[...], stack, preferred_element_type=jnp.float32)
            lifted = jnp.concatenate(
                [lift_w * window[o + 6 : o + 7] + lift_b for o in range(8)], axis=0
            )
            value = lifted + jnp.maximum(mixed + bias, 0.0)
            feat1[pl.ds(target, 8 * channels), LANES + start : LANES + start + chunk] = (
                value.astype(jnp.bfloat16)
            )
            if start == 0:
                ends["low"] = value[:, :LANES]
            if start + chunk == width:
                ends["top"] = value[:, chunk - LANES :]
        store_edges(feat1, pl.ds(target, 8 * channels), ends["low"], ends["top"])

    def layer_rows(ref, weights_ref, bias, source, start):
        depth = (ROWS_DOT + 2) * channels
        parts = [
            ref[pl.ds(source, depth), start + j * LANES : start + j * LANES + chunk]
            for j in range(3)
        ]
        centre = parts[1].astype(jnp.float32)[channels : (ROWS_DOT + 1) * channels]
        stack = jnp.concatenate(parts, axis=0)
        mixed = jnp.dot(weights_ref[...], stack, preferred_element_type=jnp.float32)
        return centre + jnp.maximum(mixed + bias, 0.0)

    span = ROWS_DOT * channels

    def second_group(group):
        target = pl.multiple_of(group * span, 16)
        bias = params_ref[:span, 4:5]
        ends = {}
        for start in range(0, width, chunk):
            value = layer_rows(feat1, second_ref, bias, target, start)
            feat2[pl.ds(target, span), LANES + start : LANES + start + chunk] = value.astype(
                jnp.bfloat16
            )
            if start == 0:
                ends["low"] = value[:, :LANES]
            if start + chunk == width:
                ends["top"] = value[:, chunk - LANES :]
        store_edges(feat2, pl.ds(target, span), ends["low"], ends["top"])

    def third_group(frame, group):
        base = pl.multiple_of(frame * high + PAD + group * 8, 8)
        target = pl.multiple_of(frame * rows + group * 8, 8)
        bias = params_ref[:span, 5:6]
        out_weight = params_ref[:span, 2:3]
        for start in range(0, width, chunk):
            sums = []
            for half in range(8 // ROWS_DOT):
                source = pl.multiple_of(group * (8 * channels) + half * span, 16)
                value = layer_rows(feat2, third_ref, bias, source, start) * out_weight
                sums.append(jnp.sum(value.reshape(ROWS_DOT, channels, chunk), axis=1))
            projected = jnp.concatenate(sums, axis=0) if len(sums) > 1 else sums[0]
            movie = frames_buf[pl.ds(base, 8), LANES + start : LANES + start + chunk]
            den_buf[pl.ds(target, 8), start : start + chunk] = movie + projected

    groups2 = -(-(rows + 2) // ROWS_DOT)
    zero_from = groups1 * 8 * channels
    if feat1.shape[0] > zero_from:
        feat1[zero_from:, :] = jnp.zeros((feat1.shape[0] - zero_from, feat1.shape[1]), jnp.bfloat16)

    def one_frame(frame, carry):
        def run1(group, inner):
            first_group(frame, group)
            return inner

        lax.fori_loop(0, groups1, run1, 0, unroll=3 if groups1 % 3 == 0 else 1)

        @pl.when(tile_index == 0)
        def _():
            feat1[0 : 2 * channels, :] = jnp.zeros((2 * channels, feat1.shape[1]), jnp.bfloat16)

        @pl.when(tile_index == tile_count - 1)
        def _():
            lower = (rows + 2) * channels
            feat1[lower : lower + 2 * channels, :] = jnp.zeros(
                (2 * channels, feat1.shape[1]), jnp.bfloat16
            )

        def run2(group, inner):
            second_group(group)
            return inner

        lax.fori_loop(0, groups2, run2, 0, unroll=3 if groups2 % 3 == 0 else 1)

        def clear(lower, count):
            first = lower // 16 * 16
            size = -(-(lower + count) // 16) * 16 - first
            at = lax.broadcasted_iota(jnp.int32, (size, feat2.shape[1]), 0) + first
            old = feat2[first : first + size, :].astype(jnp.float32)
            outside = (at >= lower) & (at < lower + count)
            feat2[first : first + size, :] = jnp.where(outside, 0.0, old).astype(jnp.bfloat16)

        @pl.when(tile_index == 0)
        def _():
            clear(0, channels)

        @pl.when(tile_index == tile_count - 1)
        def _():
            clear((rows + 1) * channels, channels)

        def run3(group, inner):
            third_group(frame, group)
            return inner

        lax.fori_loop(0, rows // 8, run3, 0, unroll=2)
        return carry

    lax.fori_loop(0, frames, one_frame, 0)
    restored = lax.dot_general(
        den_buf[...].astype(jnp.bfloat16),
        perm_ref[...],
        (((1,), (1,)), ((), ())),
        preferred_element_type=jnp.float32,
    )
    result_ref[...] = restored.astype(jnp.bfloat16).reshape(frames, rows, width)


def halo_kernel(movie_ref, low_ref, top_ref, from_low, from_top, send_sem, recv_sem):
    me_tm = lax.axis_index("tm")
    me = lax.axis_index("tile")
    count = lax.axis_size("tile")
    rows = movie_ref.shape[1]
    above = lax.rem(me + count - 1, count)
    below = lax.rem(me + 1, count)
    barrier = pltpu.get_barrier_semaphore()
    for other in (above, below):
        pl.semaphore_signal(
            barrier, inc=1, device_id=(me_tm, other), device_id_type=pl.DeviceIdType.MESH
        )
    pl.semaphore_wait(barrier, 2)
    down = pltpu.make_async_remote_copy(
        src_ref=movie_ref.at[:, rows - HALO :],
        dst_ref=from_low,
        send_sem=send_sem.at[0],
        recv_sem=recv_sem.at[0],
        device_id=(me_tm, below),
        device_id_type=pl.DeviceIdType.MESH,
    )
    up = pltpu.make_async_remote_copy(
        src_ref=movie_ref.at[:, :HALO],
        dst_ref=from_top,
        send_sem=send_sem.at[1],
        recv_sem=recv_sem.at[1],
        device_id=(me_tm, above),
        device_id_type=pl.DeviceIdType.MESH,
    )
    down.start()
    up.start()
    down.wait()
    up.wait()
    low_ref[...] = from_low[...]
    top_ref[...] = from_top[...]


def denoise(movie, lift_weight, lift_bias, depth_kernel, mix_weight, mix_bias, out_weight):
    frames, rows, width = movie.shape
    channels = lift_weight.shape[0]
    vmem = pl.BlockSpec(memory_space=pltpu.VMEM)
    band = jax.ShapeDtypeStruct((frames, HALO, width), movie.dtype)
    low, top = pl.pallas_call(
        halo_kernel,
        out_shape=(band, band),
        in_specs=[vmem],
        out_specs=(vmem, vmem),
        scratch_shapes=[
            pltpu.VMEM(band.shape, band.dtype),
            pltpu.VMEM(band.shape, band.dtype),
            pltpu.SemaphoreType.DMA((2,)),
            pltpu.SemaphoreType.DMA((2,)),
        ],
        compiler_params=pltpu.CompilerParams(collective_id=1, has_side_effects=True),
    )(movie)
    blank = jnp.zeros((2, channels), jnp.float32)
    gap = jnp.zeros((LAYERS, 7, channels), jnp.float32)
    taps = jnp.concatenate([depth_kernel.transpose(0, 2, 1), gap], axis=1)
    vectors = jnp.concatenate(
        [
            lift_weight[None],
            lift_bias[None],
            out_weight[None],
            mix_bias,
            blank,
            taps.reshape(LAYERS * 16, channels),
        ],
        axis=0,
    )
    groups1 = (rows + 2 * (LAYERS - 1) + 7) // 8
    groups2 = -(-(rows + 2) // ROWS_DOT)
    rows1 = max(groups1 * 8, groups2 * ROWS_DOT + 2)
    rows2 = groups2 * ROWS_DOT
    wide = width + 2 * LANES
    high = rows + 2 * PAD
    return pl.pallas_call(
        denoise_kernel,
        out_shape=jax.ShapeDtypeStruct(movie.shape, jnp.bfloat16),
        in_specs=[vmem] * 5,
        out_specs=pl.BlockSpec(memory_space=pltpu.VMEM),
        scratch_shapes=[
            pltpu.VMEM((width, width), jnp.bfloat16),
            pltpu.VMEM((8 * channels, 192), jnp.bfloat16),
            pltpu.VMEM((ROWS_DOT * channels, 3 * (ROWS_DOT + 2) * channels), jnp.bfloat16),
            pltpu.VMEM((ROWS_DOT * channels, 3 * (ROWS_DOT + 2) * channels), jnp.bfloat16),
            pltpu.VMEM((8 * channels, 8), jnp.float32),
            pltpu.VMEM((frames * high, wide), jnp.float32),
            pltpu.VMEM((high, wide), jnp.float32),
            pltpu.VMEM((rows1 * channels, wide), jnp.bfloat16),
            pltpu.VMEM((rows2 * channels, wide), jnp.bfloat16),
            pltpu.VMEM((frames * rows, width), jnp.float32),
        ],
        compiler_params=pltpu.CompilerParams(vmem_limit_bytes=40 * 1024 * 1024),
    )(
        movie,
        low,
        top,
        vectors,
        mix_weight,
    )


def trace_kernel(
    slot_capacity,
    denoised_ref,
    taps_ref,
    footprints_ref,
    slots_ref,
    filtered_ref,
    traces_ref,
    received,
    padded,
    filtered_rows,
    filtered_flat,
    feet,
    feet_rows,
    feet_flat,
    outgoing,
    arriving,
    load_sem,
    own_sems,
    frame_send,
    frame_recv,
    trace_send,
    trace_recv,
):
    me_tm = lax.axis_index("tm")
    me_tile = lax.axis_index("tile")
    tm_count = lax.axis_size("tm")
    tile_count = lax.axis_size("tile")
    count = tm_count * tile_count
    me = me_tm * tile_count + me_tile
    frames = denoised_ref.shape[0]
    slots, rows, cols = feet.shape
    total, _, _ = received.shape
    half = taps_ref.shape[0] // 2

    load = pltpu.make_async_copy(footprints_ref, feet, load_sem)
    load.start()
    barrier = pltpu.get_barrier_semaphore()

    def greet(offset, carry):
        other = lax.rem(me + offset, count)
        pl.semaphore_signal(
            barrier,
            inc=1,
            device_id=(other // tile_count, lax.rem(other, tile_count)),
            device_id_type=pl.DeviceIdType.MESH,
        )
        return carry

    lax.fori_loop(1, count, greet, 0)
    pl.semaphore_wait(barrier, count - 1)

    def frame_copy(offset):
        other = lax.rem(me_tm + offset, tm_count)
        return pltpu.make_async_remote_copy(
            src_ref=denoised_ref.at[:, :, pl.ds(pl.multiple_of(other * cols, cols), cols)],
            dst_ref=received.at[pl.ds(me_tm * frames, frames)],
            send_sem=frame_send.at[offset],
            recv_sem=frame_recv.at[offset],
            device_id=(other, me_tile),
            device_id_type=pl.DeviceIdType.MESH,
        )

    own = pltpu.make_async_copy(
        denoised_ref.at[:, :, pl.ds(pl.multiple_of(me_tm * cols, cols), cols)],
        received.at[pl.ds(me_tm * frames, frames)],
        own_sems.at[0],
    )
    own.start()
    for offset in range(1, tm_count):
        frame_copy(offset).start()

    load.wait()

    def widen(block, carry):
        at = pl.multiple_of(block * 8, 8)
        feet_rows[pl.ds(pl.multiple_of(block * (8 * rows), 8 * rows), 8 * rows), :] = (
            feet[pl.ds(at, 8)].astype(jnp.float32).reshape(8 * rows, cols)
        )
        return carry

    lax.fori_loop(0, slots // 8, widen, 0, unroll=4)

    def flatten(row, carry):
        at = pl.multiple_of(row * cols, cols)
        feet_flat[:, pl.ds(at, cols)] = feet_rows[pl.ds(row, slots, stride=rows), :].astype(
            jnp.bfloat16
        )
        return carry

    lax.fori_loop(0, rows, flatten, 0, unroll=4)

    owner = slots_ref[:, 0:1]
    device = lax.broadcasted_iota(jnp.int32, (slots, count), 1)
    chosen = jnp.where(owner == device, 1.0, 0.0)
    earlier = jnp.dot(
        one_hot((slots, slots), lambda s, other: other < s).astype(jnp.bfloat16),
        chosen.astype(jnp.bfloat16),
        preferred_element_type=jnp.float32,
    )
    rank = jnp.sum(earlier * chosen, axis=1, keepdims=True)
    place = owner.astype(jnp.float32) * float(slot_capacity) + rank
    spot = lax.broadcasted_iota(jnp.int32, (slots, count * slot_capacity), 1).astype(jnp.float32)
    packing = jnp.where(place == spot, 1.0, 0.0).astype(jnp.bfloat16)
    neuron = slots_ref[:, 1:2]
    digits_high = (neuron // 16).astype(jnp.float32)
    digits_low = (neuron % 16).astype(jnp.float32)

    for edge in (0, half + total):
        padded[edge : edge + half] = jnp.zeros((half, rows, cols), jnp.float32)
    own.wait()
    for offset in range(1, tm_count):
        frame_copy(offset).wait()

    def unpack(frame, carry):
        padded[frame + half] = received[frame].astype(jnp.float32)
        return carry

    lax.fori_loop(0, total, unpack, 0, unroll=4)
    taps = [taps_ref[tap] for tap in range(2 * half + 1)]

    def filter_frame(frame, carry):
        summed = taps[0] * padded[frame]
        for tap in range(1, 2 * half + 1):
            summed = summed + taps[tap] * padded[frame + tap]
        rounded = summed.astype(jnp.bfloat16)
        filtered_ref[frame] = rounded
        filtered_rows[pl.ds(pl.multiple_of(frame * rows, rows), rows), :] = rounded.astype(
            jnp.float32
        )
        return carry

    lax.fori_loop(0, total, filter_frame, 0, unroll=2)

    def flatten_frames(row, carry):
        at = pl.multiple_of(row * cols, cols)
        filtered_flat[:, pl.ds(at, cols)] = filtered_rows[
            pl.ds(row, total, stride=rows), :
        ].astype(jnp.bfloat16)
        return carry

    lax.fori_loop(0, rows, flatten_frames, 0, unroll=4)
    partial_value = lax.dot_general(
        feet_flat[...],
        filtered_flat[...],
        (((1,), (1,)), ((), ())),
        preferred_element_type=jnp.float32,
    )
    lane = lax.broadcasted_iota(jnp.int32, (slots, LANES), 1)
    wide = jnp.concatenate(
        [partial_value, jnp.zeros((slots, LANES - total), jnp.float32)], axis=1
    )
    wide = jnp.where(lane == total, digits_high, jnp.where(lane == total + 1, digits_low, wide))
    packed = lax.dot_general(
        packing,
        wide.astype(jnp.bfloat16),
        (((0,), (0,)), ((), ())),
        preferred_element_type=jnp.float32,
    )
    outgoing[...] = packed.astype(jnp.bfloat16).reshape(count, slot_capacity, LANES)

    def trace_copy(offset):
        other = lax.rem(me + offset, count)
        return pltpu.make_async_remote_copy(
            src_ref=outgoing.at[other],
            dst_ref=arriving.at[me],
            send_sem=trace_send.at[offset],
            recv_sem=trace_recv.at[offset],
            device_id=(other // tile_count, lax.rem(other, tile_count)),
            device_id_type=pl.DeviceIdType.MESH,
        )

    def send(offset, carry):
        trace_copy(offset).start()
        return carry

    lax.fori_loop(1, count, send, 0)
    own_traces = pltpu.make_async_copy(outgoing.at[me], arriving.at[me], own_sems.at[1])
    own_traces.start()
    own_traces.wait()

    def finish(offset, carry):
        trace_copy(offset).wait()
        return carry

    lax.fori_loop(1, count, finish, 0)
    gathered = arriving[...].reshape(count * slot_capacity, LANES)
    digits = gathered.astype(jnp.float32)
    index = digits[:, total : total + 1] * 16.0 + digits[:, total + 1 : total + 2]
    neurons = traces_ref.shape[0]
    wanted = lax.broadcasted_iota(jnp.int32, (count * slot_capacity, neurons), 1)
    member = jnp.where(index == wanted.astype(jnp.float32), 1.0, 0.0).astype(jnp.bfloat16)
    summed = lax.dot_general(
        member, gathered, (((0,), (0,)), ((), ())), preferred_element_type=jnp.float32
    )
    traces_ref[...] = summed[:, :total]


def local(
    movie,
    lift_weight,
    lift_bias,
    depth_kernel,
    mix_weight,
    mix_bias,
    out_weight,
    temporal_kernel,
    footprints,
    slot_owner,
    slot_neuron,
):
    denoised = denoise(
        movie, lift_weight, lift_bias, depth_kernel, mix_weight, mix_bias, out_weight
    )
    tm_count = lax.axis_size("tm")
    count = tm_count * lax.axis_size("tile")
    frames, rows, _ = movie.shape
    slots, _, cols = footprints.shape
    total = frames * tm_count
    slot_capacity = max(16, 2 * slots // count)
    half = temporal_kernel.shape[0] // 2
    vmem = pl.BlockSpec(memory_space=pltpu.VMEM)
    filtered, traces = pl.pallas_call(
        functools.partial(trace_kernel, slot_capacity),
        out_shape=(
            jax.ShapeDtypeStruct((total, rows, cols), jnp.bfloat16),
            jax.ShapeDtypeStruct((NEUR_DEV, total), jnp.float32),
        ),
        in_specs=[
            vmem,
            pl.BlockSpec(memory_space=pltpu.SMEM),
            pl.BlockSpec(memory_space=pl.ANY),
            vmem,
        ],
        out_specs=(vmem, vmem),
        scratch_shapes=[
            pltpu.VMEM((total, rows, cols), jnp.bfloat16),
            pltpu.VMEM((total + 2 * half, rows, cols), jnp.float32),
            pltpu.VMEM((total * rows, cols), jnp.float32),
            pltpu.VMEM((total, rows * cols), jnp.bfloat16),
            pltpu.VMEM((slots, rows, cols), jnp.bfloat16),
            pltpu.VMEM((slots * rows, cols), jnp.float32),
            pltpu.VMEM((slots, rows * cols), jnp.bfloat16),
            pltpu.VMEM((count, slot_capacity, LANES), jnp.bfloat16),
            pltpu.VMEM((count, slot_capacity, LANES), jnp.bfloat16),
            pltpu.SemaphoreType.DMA,
            pltpu.SemaphoreType.DMA((2,)),
            pltpu.SemaphoreType.DMA((tm_count,)),
            pltpu.SemaphoreType.DMA((tm_count,)),
            pltpu.SemaphoreType.DMA((count,)),
            pltpu.SemaphoreType.DMA((count,)),
        ],
        compiler_params=pltpu.CompilerParams(
            collective_id=0, has_side_effects=True, vmem_limit_bytes=44 * 1024 * 1024
        ),
    )(
        denoised,
        temporal_kernel,
        footprints,
        jnp.concatenate([slot_owner, slot_neuron[:, None]], axis=1),
    )
    return (filtered, traces)


def solution(mesh):
    return jax.shard_map(
        local,
        mesh=mesh,
        in_specs=(
            P("tm", "tile", None),
            P(),
            P(),
            P(),
            P(),
            P(),
            P(),
            P(),
            P(None, "tile", "tm"),
            P(("tm", "tile"), None),
            P(("tm", "tile")),
        ),
        out_specs=(P(None, "tile", "tm"), P(("tm", "tile"), None)),
        check_vma=False,
    )
```
